768 devices in a mesh: grp: 32 (over x, y), rep: 24 (over z, core).
Axes of the slice: x: 4, y: 8, z: 12, core: 2. Of those that a mesh axis runs over, the one named last changes fastest.
Arguments:
- pooled_grad: bfloat16 [786432, 256], P(('grp', 'rep')), may hold values from -6 to 6
- lookup_bag: int32 [768, 2048], P(('grp', 'rep')), may hold values from 0 to 1023, never falling along the last dimension, each value on 1 to 8 neighbouring positions
- saved_quotient: bfloat16 [1572864, 256], P(('grp', 'rep')), may hold values from -6 to 6
- saved_remainder: bfloat16 [1572864, 256], P(('grp', 'rep')), may hold values from -6 to 6
- quotient_slot: int32 [768, 2048], P(('grp', 'rep')), may hold values from 0 to 1535
- quotient_rows: int32 [768, 1536], P(('grp', 'rep')), may hold values from 0 to 255
- remainder_slot: int32 [768, 2048], P(('grp', 'rep')), may hold values from 0 to 511
- remainder_rows: int32 [768, 512], P(('grp', 'rep')), may hold values from 0 to 63
- tower_inputs: bfloat16 [98304, 512], P(('grp', 'rep')), may hold values from -6 to 6
- tower_cotangent: bfloat16 [98304, 256], P(('grp', 'rep')), may hold values from -0.01953125 to 0.01953125
Outputs:
- quotient_grad: float32 [196608, 256], P(('grp', 'rep'))
- remainder_grad: float32 [2048, 256], P('grp')
- tower_grad: float32 [512, 256], replicated
The draws below stay inside these ranges and needn't reach their ends.
Inputs may be any that keep to these rules, and one draw needn't show every extreme that they name: `lookup_bag`: along each device's row the bag number never falls and each of the 1024 bags holds 1 to 8 lookups. `quotient_slot`: slot s belongs to the owner device with number s // 2. `remainder_slot`: slot s belongs to the owners with grp index s // 16.
All inputs are finite; a program needn't handle non-finite values.
Results may differ from the reference program's by a relative error of at most 0.0003.
Values sent between devices are 32-bit elements; how exact they have to be, the bound alone decides.
No kernel may reach another device: no remote copies, remote signals or barrier semaphores. Data moves between devices by JAX's collectives and lax.ppermute only.
A program may use at most 32 MiB of HBM per device.

```python
import math
import jax
import jax.numpy as jnp
import numpy as np
from jax import lax

E = 256
HID_IN = 512
HID_OUT = 256
B_DEV = 128
BAG_MOST = 8
CAPQ = 2
CAPR = 16
QROWS_DEV = 256
RROWS_DEV = 64
BAGS_DEV = 1024
LOOK_DEV = 2048
QSLOTS = 1536
RSLOTS = 512
N_GRP = 32
DEVICES = 768


def with_ends(array, rng, smallest, high):
    dims = array.shape
    index_at = [jax.random.randint(jax.random.fold_in(rng, axis), (), 0, dims[axis]) for axis in range(len(dims))]
    array = array.at[tuple(index_at)].set(smallest)
    longest = dims.index(max(dims))
    index_at[longest] = (index_at[longest] + 1) % dims[longest]
    return array.at[tuple(index_at)].set(high)


def block_levels(own_key, dims, split, smallest, high):
    gain = 1.0
    for position, shards_of in split:
        heights = jax.random.uniform(jax.random.fold_in(jax.random.fold_in(own_key, 6), position), (shards_of,), jnp.float32, smallest / len(split), high / len(split))
        gain = gain * jnp.repeat(jnp.exp(heights), dims[position] // shards_of).reshape((-1,) + (1,) * (len(dims) - 1 - position))
    return gain


def rank_table(number_of, lean):
    portions = [(1 << 20) // math.isqrt(grade ** lean) + 1 for grade in range(1, number_of + 1)]
    scale = 1 + sum(portions) // (1 << 30)
    return np.cumsum(np.array([max(1, weight // scale) for weight in portions]))


def ranked_ids(rng, shape, count, lean):
    grid = rank_table(count, lean)
    lot = jax.random.randint(jax.random.fold_in(rng, 1), shape, 0, int(grid[count - 1]))
    rank = jnp.searchsorted(jnp.asarray(grid, jnp.int32), lot, side="right")
    return jax.random.permutation(jax.random.fold_in(rng, 2), count)[rank].astype(jnp.int32)


def length_profile(amount, total, bound, lean):
    portions = [(1 << 20) // math.isqrt(standing ** lean) + 1 for standing in range(2, amount + 1)]
    surplus, counts = total - bound - (amount - 1), [1] * (amount - 1)
    while surplus > 0:
        movable = [i for i in range(amount - 1) if counts[i] < bound]
        whole, left = sum([portions[i] for i in movable]), surplus
        for i in movable:
            more = min(bound - counts[i], max(1, left * portions[i] // whole), surplus)
            counts[i] = counts[i] + more
            surplus = surplus - more
    return np.array([bound] + counts)


def ragged_sizes(key, amount, total, limit, skew):
    if amount == 2:
        one = jax.random.randint(key, (), max(1, total - limit), min(limit, total - 1) + 1)
        return jnp.stack([one, total - one])
    sizes = jnp.asarray(length_profile(amount, total, limit, skew), jnp.int32)
    couples = (amount - 1) // 2
    giver, sink = sizes[1:1 + 2 * couples:2], sizes[2:2 + 2 * couples:2]
    margin = jnp.minimum(giver - 1, limit - sink)
    moved = jax.random.randint(jax.random.fold_in(key, 1), (couples,), 0, 1 << 20) % (margin + 1)
    sizes = sizes.at[1:1 + 2 * couples:2].set(giver - moved).at[2:2 + 2 * couples:2].set(sink + moved)
    return sizes[jax.random.permutation(jax.random.fold_in(key, 2), amount)]


def normal_values(key, dims, spread, most, cuts=(), held_as=jnp.bfloat16):
    values = spread * jax.random.normal(key, dims, jnp.float32)
    if cuts:
        values = values * block_levels(key, dims, cuts, -0.22, 0.18)
    return jnp.clip(values, -most, most).astype(held_as)


def setup_inputs(seed: int = 0) -> dict:
    streams_of = jax.random.split(jax.random.key(seed), 11)
    pooled_grad = normal_values(streams_of[0], (BAGS_DEV * DEVICES, E), 1.0, 6.0, ((0, 768),))
    lookup_bag = jax.vmap(lambda own: jnp.searchsorted(jnp.cumsum(ragged_sizes(own, BAGS_DEV, LOOK_DEV, BAG_MOST, 2)), jnp.arange(LOOK_DEV), side="right"))(jax.random.split(streams_of[1], DEVICES)).reshape((DEVICES, LOOK_DEV)).astype(jnp.int32)
    saved_quotient = normal_values(streams_of[2], (DEVICES * LOOK_DEV, E), 1.0, 6.0, ((0, 768),))
    saved_remainder = normal_values(streams_of[3], (DEVICES * LOOK_DEV, E), 1.0, 6.0, ((0, 768),))
    quotient_slot = with_ends(ranked_ids(streams_of[4], (DEVICES, LOOK_DEV), QSLOTS, 1), jax.random.fold_in(streams_of[4], 3), 0, QSLOTS - 1).astype(jnp.int32)
    quotient_rows = with_ends(jax.random.randint(streams_of[5], (DEVICES, QSLOTS), 0, QROWS_DEV), jax.random.fold_in(streams_of[5], 1), 0, QROWS_DEV - 1).astype(jnp.int32)
    remainder_slot = with_ends(jax.random.randint(streams_of[6], (DEVICES, LOOK_DEV), 0, RSLOTS), jax.random.fold_in(streams_of[6], 1), 0, RSLOTS - 1).astype(jnp.int32)
    remainder_rows = with_ends(jax.random.randint(streams_of[7], (DEVICES, RSLOTS), 0, RROWS_DEV), jax.random.fold_in(streams_of[7], 1), 0, RROWS_DEV - 1).astype(jnp.int32)
    tower_inputs = normal_values(streams_of[8], (B_DEV * DEVICES, HID_IN), 1.0, 6.0, ((0, 768),))
    tower_cotangent = normal_values(streams_of[9], (B_DEV * DEVICES, HID_OUT), (B_DEV * DEVICES) ** -0.5, 0.01953125, ((0, 768),))
    return {"pooled_grad": pooled_grad, "lookup_bag": lookup_bag, "saved_quotient": saved_quotient, "saved_remainder": saved_remainder, "quotient_slot": quotient_slot, "quotient_rows": quotient_rows, "remainder_slot": remainder_slot, "remainder_rows": remainder_rows, "tower_inputs": tower_inputs, "tower_cotangent": tower_cotangent}


def reference(pooled_grad, lookup_bag, saved_quotient, saved_remainder, quotient_slot, quotient_rows, remainder_slot, remainder_rows, tower_inputs, tower_cotangent):
    pooled = pooled_grad.reshape(DEVICES, BAGS_DEV, E)
    saved_q = saved_quotient.reshape(DEVICES, LOOK_DEV, E)
    saved_r = saved_remainder.reshape(DEVICES, LOOK_DEV, E)
    quotient_owner = (jnp.arange(QSLOTS, dtype=jnp.int32) // CAPQ) * QROWS_DEV
    remainder_owner = (jnp.arange(RSLOTS, dtype=jnp.int32) // CAPR) * RROWS_DEV

    def device_step(tables, slices):
        quotient_table, remainder_table = tables
        pooled_dev, bag_index, quot_dev, rem_dev, quot_slots, quot_rows, rem_slots, rem_rows = slices
        gathered = pooled_dev[bag_index].astype(jnp.float32)
        quotient_terms = gathered * rem_dev.astype(jnp.float32)
        remainder_terms = gathered * quot_dev.astype(jnp.float32)
        quotient_sums = jax.ops.segment_sum(quotient_terms, quot_slots, num_segments=QSLOTS)
        remainder_sums = jax.ops.segment_sum(remainder_terms, rem_slots, num_segments=RSLOTS)
        quotient_table = quotient_table.at[quotient_owner + quot_rows].add(quotient_sums)
        remainder_table = remainder_table.at[remainder_owner + rem_rows].add(remainder_sums)
        return (quotient_table, remainder_table), None

    start_tables = (jnp.zeros((QROWS_DEV * DEVICES, E), jnp.float32), jnp.zeros((RROWS_DEV * N_GRP, E), jnp.float32))
    (quotient_grad, remainder_grad), _ = lax.scan(device_step, start_tables, (pooled, lookup_bag, saved_q, saved_r, quotient_slot, quotient_rows, remainder_slot, remainder_rows))
    tower_grad = jnp.dot(tower_inputs.T, tower_cotangent, preferred_element_type=jnp.float32)
    return quotient_grad, remainder_grad, tower_grad
```

```python
import jax
import jax.numpy as jnp
from jax import lax
from jax.experimental import pallas as pl
from jax.experimental.pallas import tpu as pltpu
from jax.sharding import Mesh
from jax.sharding import PartitionSpec as P

E = 256
LANES = 128
LOOK = 2048
BAGS = 1024
QCAP = 2
RCAP = 16
QROWS = 256
RROWS = 64
NX, NY, NZ, NC = 4, 8, 12, 2
GRP = NX * NY
DEVICES = GRP * NZ * NC
HID = 512
TROWS = HID // GRP
PIECE = 72
MESSAGE = 5
F32 = jnp.float32
BF16 = jnp.bfloat16
AXES = ("x", "y", "z", "c")
VMEM = pl.BlockSpec(memory_space=pltpu.VMEM)
SMEM = pl.BlockSpec(memory_space=pltpu.SMEM)


def call(body, out_shape, inputs, specs, scratch=(), flops=0, nbytes=0):
    return pl.pallas_call(
        body,
        out_shape=out_shape,
        in_specs=specs,
        out_specs=jax.tree.map(lambda _: VMEM, out_shape),
        scratch_shapes=list(scratch),
        compiler_params=pltpu.CompilerParams(vmem_limit_bytes=32 * 1024 * 1024),
        cost_estimate=pl.CostEstimate(flops=flops, bytes_accessed=nbytes, transcendentals=0),
    )(*inputs)


def split_terms(bag_smem, bag_ref, pooled_ref, saved_ref, parts_ref):
    lane = lax.broadcasted_iota(jnp.int32, (LANES, LANES), 1)
    for block in range(LOOK // LANES):
        rows = pl.ds(block * LANES, LANES)
        first = jnp.minimum(bag_smem[0, block * LANES] // 16 * 16, BAGS - 2 * LANES)
        first = pl.multiple_of(first, 16)
        row = bag_ref[0:1, block * LANES : (block + 1) * LANES] - first
        column = jnp.transpose(jnp.broadcast_to(row, (LANES, LANES)).astype(F32)).astype(jnp.int32)
        pick = jnp.concatenate([column == lane, column == lane + LANES], axis=1)
        pick = jnp.where(pick, 1.0, 0.0).astype(BF16)
        gathered = jnp.dot(pick, pooled_ref[pl.ds(first, 2 * LANES), :], preferred_element_type=F32)
        terms = gathered * saved_ref[rows, :].astype(F32)
        high = terms.astype(BF16)
        parts_ref[rows, 0:E] = high
        parts_ref[rows, E:] = (terms - high.astype(F32)).astype(BF16)


def one_hot(index_row, first, count, step=1):
    number = lax.broadcasted_iota(jnp.int32, (count, index_row.shape[1]), 0) * step + first
    return jnp.where(number == index_row, 1.0, 0.0).astype(BF16)


def sums(pick, parts):
    both = jnp.dot(pick, parts, preferred_element_type=F32)
    return both[:, :E] + both[:, E:]


def small_kernel(bag_smem, bag_ref, pooled_ref, saved_ref, slot_ref, rows_ref, tin_ref, tcot_ref, out_ref, parts_ref):
    tower = lax.dot_general(tin_ref[...], tcot_ref[...], (((0,), (0,)), ((), ())), preferred_element_type=F32)
    tower = tower.reshape(GRP, TROWS, E)
    out_ref[:, 32:48, :] = tower[:, :, :LANES]
    out_ref[:, 48:64, :] = tower[:, :, LANES:]
    labels = jnp.broadcast_to(rows_ref[...], (GRP, GRP * RCAP))
    slot = lax.broadcasted_iota(jnp.int32, (GRP, GRP * RCAP), 1)
    group = lax.broadcasted_iota(jnp.int32, (GRP, GRP * RCAP), 0)
    labels = jnp.where(slot // RCAP == group, labels, 0).astype(F32).astype(BF16)
    slot = lax.broadcasted_iota(jnp.int32, (GRP * RCAP, LANES), 0)
    lane = lax.broadcasted_iota(jnp.int32, (GRP * RCAP, LANES), 1)
    spread = jnp.where(slot % RCAP == lane % RCAP, 1.0, 0.0).astype(BF16)
    labels = jnp.dot(labels, spread, preferred_element_type=F32)
    out_ref[:, 64:72, :] = jnp.broadcast_to(labels[:, None, :], (GRP, 8, LANES))
    split_terms(bag_smem, bag_ref, pooled_ref, saved_ref, parts_ref)
    slots = slot_ref[...]
    for half in range(2):
        found = sums(one_hot(slots, half * 256, 256), parts_ref[...]).reshape(GRP // 2, RCAP, E)
        groups = pl.ds(half * (GRP // 2), GRP // 2)
        out_ref[groups, 0:16, :] = found[:, :, :LANES]
        out_ref[groups, 16:32, :] = found[:, :, LANES:]


def large_kernel(bag_smem, bag_ref, pooled_ref, saved_ref, slot_ref, label_ref, out_ref, parts_ref):
    split_terms(bag_smem, bag_ref, pooled_ref, saved_ref, parts_ref)
    slots = slot_ref[...]
    chunk = 256
    for block in range(DEVICES // chunk):
        base = block * chunk * MESSAGE
        for p in range(QCAP):
            found = sums(one_hot(slots, block * chunk * QCAP + p, chunk, QCAP), parts_ref[...])
            for h in range(2):
                out_ref[pl.ds(base + 2 * p + h, chunk, stride=MESSAGE), :] = found[:, h * LANES : (h + 1) * LANES]
        out_ref[pl.ds(base + 4, chunk, stride=MESSAGE), :] = label_ref[pl.ds(block * chunk, chunk), :]


def halves(values):
    high = values.astype(BF16)
    return jnp.concatenate([high, (values - high.astype(F32)).astype(BF16)], axis=1)


def merge_kernel(got_ref, out_ref):
    source = lax.broadcasted_iota(jnp.int32, (8, 8, LANES), 0)
    lane = lax.broadcasted_iota(jnp.int32, (8, 8, LANES), 2)
    labels = []
    for k in range(GRP // 8):
        rows = jnp.where(lane // RCAP == source, got_ref[8 * k : 8 * k + 8, 64:72, :], 0.0)
        labels.append(jnp.sum(rows, axis=0)[0:1, :])
    pick = one_hot(jnp.concatenate(labels, axis=1).astype(jnp.int32), 0, RROWS)
    for h in range(2):
        values = got_ref[:, 16 * h : 16 * h + 16, :].reshape(GRP * RCAP, LANES)
        both = jnp.dot(pick, halves(values), preferred_element_type=F32)
        out_ref[h, 0:64, :] = both[:, :LANES] + both[:, LANES:]
        out_ref[h, 64:80, :] = jnp.sum(got_ref[:, 32 + 16 * h : 48 + 16 * h, :], axis=0)


def owner_kernel(got_ref, out_ref):
    labels = jnp.transpose(got_ref[pl.ds(4, DEVICES, stride=MESSAGE), :])[0:8, :].astype(jnp.int32)
    total = None
    for p in range(QCAP):
        pick = one_hot(labels[p : p + 1, :], 0, QROWS)
        values = jnp.concatenate([got_ref[pl.ds(2 * p + h, DEVICES, stride=MESSAGE), :] for h in range(2)], axis=1)
        part = sums(pick, halves(values))
        total = part if total is None else total + part
    out_ref[...] = total


def finish_kernel(own_ref, other_ref, own_rem_ref, other_rem_ref, rem_ref, tower_ref):
    group = lax.axis_index("x") * NY + lax.axis_index("y")

    def place(own, other, left, right):
        rem_ref[:, left] = own[0][...]
        rem_ref[:, right] = other[0][...]
        for j in range(GRP):
            rows = pl.ds(pl.multiple_of(jnp.bitwise_xor(group, j) * TROWS, TROWS), TROWS)
            tower_ref[rows, left] = own[1][j * TROWS : (j + 1) * TROWS, :]
            tower_ref[rows, right] = other[1][j * TROWS : (j + 1) * TROWS, :]

    low, high = slice(0, LANES), slice(LANES, E)

    @pl.when(lax.axis_index("c") == 0)
    def _():
        place((own_rem_ref, own_ref), (other_rem_ref, other_ref), low, high)

    @pl.when(lax.axis_index("c") == 1)
    def _():
        place((own_rem_ref, own_ref), (other_rem_ref, other_ref), high, low)


def shift(value, axis, size, by):
    return lax.ppermute(value, axis, [(i, (i + by) % size) for i in range(size)])


def swap(value, axis, size, bit):
    return lax.ppermute(value, axis, [(i, i ^ bit) for i in range(size)])


def local(
    pooled_grad,
    lookup_bag,
    saved_quotient,
    saved_remainder,
    quotient_slot,
    quotient_rows,
    remainder_slot,
    remainder_rows,
    tower_inputs,
    tower_cotangent,
):
    parts = pltpu.VMEM((LOOK, 2 * E), BF16)
    pieces = call(
        small_kernel,
        jax.ShapeDtypeStruct((GRP, PIECE, LANES), F32),
        (lookup_bag, lookup_bag, pooled_grad, saved_quotient, remainder_slot, remainder_rows, tower_inputs, tower_cotangent),
        [SMEM] + [VMEM] * 7,
        [parts],
        flops=2 * 10**9,
        nbytes=3 * 10**6,
    )
    got = lax.all_to_all(pieces, ("x", "y"), split_axis=0, concat_axis=0, tiled=True)
    label_rows = jnp.pad(quotient_rows.reshape(DEVICES, QCAP).astype(F32), ((0, 0), (0, LANES - QCAP)))
    outgoing = call(
        large_kernel,
        jax.ShapeDtypeStruct((DEVICES * MESSAGE, LANES), F32),
        (lookup_bag, lookup_bag, pooled_grad, saved_remainder, quotient_slot, label_rows),
        [SMEM] + [VMEM] * 5,
        [parts],
        flops=8 * 10**9,
        nbytes=5 * 10**6,
    )
    arrived = lax.all_to_all(
        outgoing.reshape(DEVICES, 1, MESSAGE * LANES), AXES, split_axis=0, concat_axis=0, tiled=True
    )
    merged = call(
        merge_kernel,
        jax.ShapeDtypeStruct((2, RROWS + TROWS, LANES), F32),
        (got,),
        [VMEM],
        flops=10**8,
        nbytes=2 * 10**6,
    )
    core = lax.axis_index("c")
    keep = lax.dynamic_index_in_dim(merged, core, 0, keepdims=False)
    give = lax.dynamic_index_in_dim(merged, 1 - core, 0, keepdims=False)
    keep = keep + swap(give, "c", NC, 1)
    keep = keep + shift(keep, "z", NZ, 1) + shift(keep, "z", NZ, -1)
    keep = keep + shift(keep, "z", NZ, 3) + shift(keep, "z", NZ, -3) + shift(keep, "z", NZ, 6)
    remainder_half, tower_half = keep[:RROWS], keep[RROWS:]
    for bit in (1, 2, 4):
        tower_half = jnp.concatenate([tower_half, swap(tower_half, "y", NY, bit)], axis=0)
    for bit in (1, 2):
        tower_half = jnp.concatenate([tower_half, swap(tower_half, "x", NX, bit)], axis=0)
    remainder_grad, tower_grad = call(
        finish_kernel,
        (jax.ShapeDtypeStruct((RROWS, E), F32), jax.ShapeDtypeStruct((HID, E), F32)),
        (tower_half, swap(tower_half, "c", NC, 1), remainder_half, swap(remainder_half, "c", NC, 1)),
        [VMEM] * 4,
        flops=10**6,
        nbytes=10**6,
    )
    quotient_grad = call(
        owner_kernel,
        jax.ShapeDtypeStruct((QROWS, E), F32),
        (arrived.reshape(DEVICES * MESSAGE, LANES),),
        [VMEM],
        flops=10**9,
        nbytes=3 * 10**6,
    )
    return (quotient_grad, remainder_grad, tower_grad)


def solution(mesh):
    fine = Mesh(mesh.devices.reshape(NX, NY, NZ, NC), AXES)
    rows = P(AXES, None)
    return jax.shard_map(
        local,
        mesh=fine,
        in_specs=(rows,) * 10,
        out_specs=(rows, P(("x", "y"), None), P()),
        check_vma=False,
    )
```

```python
import jax
import jax.numpy as jnp
from jax import lax
from jax.experimental import pallas as pl
from jax.experimental.pallas import tpu as pltpu
from jax.sharding import Mesh
from jax.sharding import PartitionSpec as P

E = 256
LANES = 128
LOOK = 2048
BAGS = 1024
QCAP = 2
RCAP = 16
QROWS = 256
RROWS = 64
NX, NY, NZ, NC = 4, 8, 12, 2
GRP = NX * NY
DEVICES = GRP * NZ * NC
HID = 512
TROWS = HID // GRP
PIECE = 72
PLANE = NX * NC
SHEET = NY * NZ
CHAIN = 96
SUMS = RROWS + TROWS
F32 = jnp.float32
BF16 = jnp.bfloat16
AXES = ("x", "y", "z", "c")
VMEM = pl.BlockSpec(memory_space=pltpu.VMEM)
SMEM = pl.BlockSpec(memory_space=pltpu.SMEM)
ANY = pl.BlockSpec(memory_space=pl.ANY)


def call(body, out_shape, inputs, specs, scratch=(), flops=0, nbytes=0, room=32):
    return pl.pallas_call(
        body,
        out_shape=out_shape,
        in_specs=specs,
        out_specs=jax.tree.map(lambda _: VMEM, out_shape),
        scratch_shapes=list(scratch),
        compiler_params=pltpu.CompilerParams(vmem_limit_bytes=room * 1024 * 1024),
        cost_estimate=pl.CostEstimate(flops=flops, bytes_accessed=nbytes, transcendentals=0),
    )(*inputs)


def split_terms(bag_smem, bag_ref, pooled_ref, saved_ref, parts_ref):
    lane = lax.broadcasted_iota(jnp.int32, (LANES, LANES), 1)
    for block in range(LOOK // LANES):
        rows = pl.ds(block * LANES, LANES)
        first = jnp.minimum(bag_smem[0, block * LANES] // 16 * 16, BAGS - 2 * LANES)
        first = pl.multiple_of(first, 16)
        row = bag_ref[0:1, block * LANES : (block + 1) * LANES] - first
        column = jnp.transpose(jnp.broadcast_to(row, (LANES, LANES)).astype(F32)).astype(jnp.int32)
        pick = jnp.concatenate([column == lane, column == lane + LANES], axis=1)
        pick = jnp.where(pick, 1.0, 0.0).astype(BF16)
        gathered = jnp.dot(pick, pooled_ref[pl.ds(first, 2 * LANES), :], preferred_element_type=F32)
        terms = gathered * saved_ref[rows, :].astype(F32)
        high = terms.astype(BF16)
        parts_ref[rows, 0:E] = high
        parts_ref[rows, E:] = (terms - high.astype(F32)).astype(BF16)


def one_hot(index_row, first, count, step=1):
    number = lax.broadcasted_iota(jnp.int32, (count, index_row.shape[1]), 0) * step + first
    return jnp.where(number == index_row, 1.0, 0.0).astype(BF16)


def sums(pick, parts):
    both = jnp.dot(pick, parts, preferred_element_type=F32)
    return both[:, :E] + both[:, E:]


def small_kernel(
    bag_smem, bag_ref, slot_ref, rows_ref, qrows_ref, pooled_hbm, saved_hbm, tin_hbm, tcot_hbm, out_ref,
    pooled_ref, saved_ref, tin_ref, tcot_ref, parts_ref, arrivals,
):
    pairs = ((tin_hbm, tin_ref), (tcot_hbm, tcot_ref), (pooled_hbm, pooled_ref), (saved_hbm, saved_ref))
    copies = [pltpu.make_async_copy(src, dst, arrivals.at[k]) for k, (src, dst) in enumerate(pairs)]
    for copy in copies:
        copy.start()
    copies[0].wait()
    copies[1].wait()
    tower = lax.dot_general(tin_ref[...], tcot_ref[...], (((0,), (0,)), ((), ())), preferred_element_type=F32)
    tower = tower.reshape(GRP, TROWS, E)
    out_ref[:, 32:48, :] = tower[:, :, :LANES]
    out_ref[:, 48:64, :] = tower[:, :, LANES:]
    labels = jnp.broadcast_to(rows_ref[...], (GRP, GRP * RCAP))
    slot = lax.broadcasted_iota(jnp.int32, (GRP, GRP * RCAP), 1)
    group = lax.broadcasted_iota(jnp.int32, (GRP, GRP * RCAP), 0)
    labels = jnp.where(slot // RCAP == group, labels, 0).astype(F32).astype(BF16)
    slot = lax.broadcasted_iota(jnp.int32, (GRP * RCAP, LANES), 0)
    lane = lax.broadcasted_iota(jnp.int32, (GRP * RCAP, LANES), 1)
    spread = jnp.where(slot % RCAP == lane % RCAP, 1.0, 0.0).astype(BF16)
    labels = jnp.dot(labels, spread, preferred_element_type=F32)
    count = DEVICES * QCAP
    slot = lax.broadcasted_iota(jnp.int32, (GRP, count), 1)
    group = lax.broadcasted_iota(jnp.int32, (GRP, count), 0)
    onward = jnp.where(slot // (count // GRP) == group, jnp.broadcast_to(qrows_ref[...], (GRP, count)), 0).astype(F32).astype(BF16)
    slot = lax.broadcasted_iota(jnp.int32, (count, LANES), 0)
    lane = lax.broadcasted_iota(jnp.int32, (count, LANES), 1)
    spread = jnp.where(slot % (count // GRP) == lane, 1.0, 0.0).astype(BF16)
    onward = jnp.dot(onward, spread, preferred_element_type=F32)
    line = lax.broadcasted_iota(jnp.int32, (GRP, 8, LANES), 1)
    out_ref[:, 64:72, :] = jnp.where(line == 0, labels[:, None, :], onward[:, None, :])
    copies[2].wait()
    copies[3].wait()
    split_terms(bag_smem, bag_ref, pooled_ref, saved_ref, parts_ref)
    slots = slot_ref[...]
    for half in range(2):
        found = sums(one_hot(slots, half * 256, 256), parts_ref[...]).reshape(GRP // 2, RCAP, E)
        groups = pl.ds(half * (GRP // 2), GRP // 2)
        out_ref[groups, 0:16, :] = found[:, :, :LANES]
        out_ref[groups, 16:32, :] = found[:, :, LANES:]


def large_kernel(bag_smem, bag_ref, pooled_ref, saved_ref, slot_ref, out_ref, parts_ref):
    split_terms(bag_smem, bag_ref, pooled_ref, saved_ref, parts_ref)
    slots = slot_ref[...]
    row = lax.broadcasted_iota(jnp.int32, (2 * SHEET, LOOK), 0)
    home = row % SHEET * 4 + row // SHEET
    for block in range(PLANE):
        first = block // NC * (4 * SHEET) + block % NC * 2
        pick = jnp.where(home == slots - first, 1.0, 0.0).astype(BF16)
        found = sums(pick, parts_ref[...])
        for h in range(2):
            out_ref[block, h * 2 * SHEET : (h + 1) * 2 * SHEET, :] = found[:, h * LANES : (h + 1) * LANES]


def turn_kernel(got_ref, out_ref):
    for source in range(PLANE):
        for h in range(2):
            for p in range(QCAP):
                rows = pl.ds(h * 16 + source * QCAP + p, SHEET, stride=32)
                first = (h * QCAP + p) * SHEET
                out_ref[rows, :] = got_ref[source, first : first + SHEET, :]


def halves(values):
    high = values.astype(BF16)
    return jnp.concatenate([high, (values - high.astype(F32)).astype(BF16)], axis=1)


def merge_kernel(got_ref, keep_ref, give_ref, onward_ref):
    source = lax.broadcasted_iota(jnp.int32, (8, 8, LANES), 0)
    lane = lax.broadcasted_iota(jnp.int32, (8, 8, LANES), 2)
    labels = []
    for k in range(GRP // 8):
        rows = jnp.where(lane // RCAP == source, got_ref[8 * k : 8 * k + 8, 64:72, :], 0.0)
        labels.append(jnp.sum(rows, axis=0)[0:1, :])
    pick = one_hot(jnp.concatenate(labels, axis=1).astype(jnp.int32), 0, RROWS)
    core = lax.axis_index("c")
    for h in range(2):
        values = got_ref[:, 16 * h : 16 * h + 16, :].reshape(GRP * RCAP, LANES)
        both = jnp.dot(pick, halves(values), preferred_element_type=F32)
        remainder = both[:, :LANES] + both[:, LANES:]
        tower = jnp.sum(got_ref[:, 32 + 16 * h : 48 + 16 * h, :], axis=0)
        for kept, ref in ((True, keep_ref), (False, give_ref)):

            @pl.when((core == h) == kept)
            def _(ref=ref, remainder=remainder, tower=tower):
                ref[0:RROWS, :] = remainder
                ref[RROWS:SUMS, :] = tower

    line = lax.broadcasted_iota(jnp.int32, (GRP, 8, LANES), 1)
    known = jnp.sum(jnp.where(line == 1, got_ref[:, 64:72, :], 0.0), axis=1).astype(BF16)
    group = lax.broadcasted_iota(jnp.int32, (GRP, LANES), 0)
    lane = lax.broadcasted_iota(jnp.int32, (GRP, LANES), 1)
    total = None
    for p in range(QCAP):
        spread = jnp.where(lane == group % NY * 16 + group // NY * 4 + core * 2 + p, 1.0, 0.0).astype(BF16)
        moved = lax.dot_general(known, spread, (((0,), (0,)), ((), ())), preferred_element_type=F32)
        row = lax.broadcasted_iota(jnp.int32, (LANES, LANES), 0)
        moved = jnp.where(row % QCAP == p, moved, 0.0)
        total = moved if total is None else total + moved
    onward_ref[...] = total
    z = lax.axis_index("z")
    for ref, c in ((keep_ref, core), (give_ref, 1 - core)):
        ref[SUMS:, :] = jnp.zeros((CHAIN - SUMS, LANES), F32)
        for i in range(NZ):
            first = lax.rem(z + i + NZ - 5, NZ) * 4 + c * 2
            at = SUMS + i % 4 * 3 + i // 4
            ref[at : at + 1, :] = onward_ref[pl.ds(first, 1), :] + onward_ref[pl.ds(first + 1, 1), :]


def near_kernel(up_ref, own_ref, down1_ref, down2_ref, out_ref):
    refs = (up_ref, own_ref, down1_ref, down2_ref)
    out_ref[0:SUMS, :] = sum(ref[0:SUMS, :] for ref in refs)
    out_ref[SUMS:, :] = jnp.zeros((CHAIN - SUMS, LANES), F32)
    for m in range(3):
        for e, ref in enumerate(refs):
            at = SUMS + 4 * m + e
            out_ref[at : at + 1, :] = ref[SUMS + 3 * e + m : SUMS + 3 * e + m + 1, :]


def pass_kernel(value_ref, after1_ref, after2_ref, out_ref):
    pass


def owner_kernel(got_ref, step0_ref, step1_ref, step2_ref, out_ref, label_ref):
    z = lax.axis_index("z")
    for m, ref in enumerate((step0_ref, step1_ref, step2_ref)):
        label_ref[4 * m : 4 * m + 4, :] = ref[SUMS + 4 * m : SUMS + 4 * m + 4, :]
    labels = [label_ref[pl.ds(lax.rem(z - source + 5 + NZ, NZ), 1), :] for source in range(NZ)]
    pick = one_hot(jnp.concatenate(labels, axis=1).astype(jnp.int32), 0, QROWS)
    for h in range(2):
        values = [
            got_ref[y * NZ + source, 16 * h : 16 * h + 16, :] for source in range(NZ) for y in range(NY)
        ]
        both = jnp.dot(pick, halves(jnp.concatenate(values, axis=0)), preferred_element_type=F32)
        out_ref[:, h * LANES : (h + 1) * LANES] = both[:, :LANES] + both[:, LANES:]


def finish_kernel(own_ref, other_ref, own_rem_ref, other_rem_ref, rem_ref, tower_ref):
    group = lax.axis_index("x") * NY + lax.axis_index("y")

    def place(own, other, left, right):
        rem_ref[:, left] = own[0][...]
        rem_ref[:, right] = other[0][...]
        for j in range(GRP):
            rows = pl.ds(pl.multiple_of(jnp.bitwise_xor(group, j) * TROWS, TROWS), TROWS)
            tower_ref[rows, left] = own[1][j * TROWS : (j + 1) * TROWS, :]
            tower_ref[rows, right] = other[1][j * TROWS : (j + 1) * TROWS, :]

    low, high = slice(0, LANES), slice(LANES, E)

    @pl.when(lax.axis_index("c") == 0)
    def _():
        place((own_rem_ref, own_ref), (other_rem_ref, other_ref), low, high)

    @pl.when(lax.axis_index("c") == 1)
    def _():
        place((own_rem_ref, own_ref), (other_rem_ref, other_ref), high, low)


def shift(value, by):
    return lax.ppermute(value, "z", [(i, (i + by) % NZ) for i in range(NZ)])


def swap(value, axis, bit):
    return lax.ppermute(value, axis, [(i, i ^ bit) for i in range(lax.axis_size(axis))])


def local(
    pooled_grad,
    lookup_bag,
    saved_quotient,
    saved_remainder,
    quotient_slot,
    quotient_rows,
    remainder_slot,
    remainder_rows,
    tower_inputs,
    tower_cotangent,
):
    parts = pltpu.VMEM((LOOK, 2 * E), BF16)
    pieces = call(
        small_kernel,
        jax.ShapeDtypeStruct((GRP, PIECE, LANES), F32),
        (lookup_bag, lookup_bag, remainder_slot, remainder_rows, quotient_rows, pooled_grad, saved_quotient, tower_inputs, tower_cotangent),
        [SMEM] + [VMEM] * 4 + [ANY] * 4,
        [
            pltpu.VMEM(pooled_grad.shape, BF16),
            pltpu.VMEM(saved_quotient.shape, BF16),
            pltpu.VMEM(tower_inputs.shape, BF16),
            pltpu.VMEM(tower_cotangent.shape, BF16),
            parts,
            pltpu.SemaphoreType.DMA((4,)),
        ],
        flops=2 * 10**9,
        nbytes=3 * 10**6,
        room=56,
    )
    got = lax.all_to_all(pieces, ("x", "y"), split_axis=0, concat_axis=0, tiled=True)
    outgoing = call(
        large_kernel,
        jax.ShapeDtypeStruct((PLANE, 4 * SHEET, LANES), F32),
        (lookup_bag, lookup_bag, pooled_grad, saved_remainder, quotient_slot),
        [SMEM] + [VMEM] * 4,
        [parts],
        flops=8 * 10**9,
        nbytes=5 * 10**6,
    )
    across = lax.all_to_all(outgoing, ("x", "c"), split_axis=0, concat_axis=0, tiled=True)

    chain = jax.ShapeDtypeStruct((CHAIN, LANES), F32)
    keep, give = call(
        merge_kernel,
        (chain, chain),
        (got,),
        [VMEM],
        [pltpu.VMEM((LANES, LANES), F32)],
        flops=10**8,
        nbytes=2 * 10**6,
    )
    keep = keep + swap(give, "c", 1)
    step = call(
        near_kernel,
        chain,
        (shift(keep, -1), keep, shift(keep, 1), shift(keep, 2)),
        [VMEM] * 4,
        flops=10**5,
        nbytes=10**5,
    )
    steps = (shift(step, -4), step, shift(step, 4))
    total = sum(value[:SUMS] for value in steps)

    turned = call(
        turn_kernel,
        jax.ShapeDtypeStruct((SHEET * 32, LANES), F32),
        (across,),
        [VMEM],
        flops=10**7,
        nbytes=4 * 10**6,
    )
    turned = pl.pallas_call(
        pass_kernel,
        out_shape=jax.ShapeDtypeStruct((SHEET * 32, LANES), F32),
        in_specs=[ANY] * 3,
        out_specs=ANY,
        input_output_aliases={0: 0},
    )(turned, steps[0], steps[2])
    arrived = lax.all_to_all(turned.reshape(SHEET, 32, LANES), ("y", "z"), split_axis=0, concat_axis=0, tiled=True)

    remainder_half, tower_half = total[:RROWS], total[RROWS:]
    for axis, bits in (("y", (1, 2, 4)), ("x", (1, 2))):
        for bit in bits:
            tower_half = jnp.concatenate([tower_half, swap(tower_half, axis, bit)], axis=0)
    remainder_grad, tower_grad = call(
        finish_kernel,
        (jax.ShapeDtypeStruct((RROWS, E), F32), jax.ShapeDtypeStruct((HID, E), F32)),
        (tower_half, swap(tower_half, "c", 1), remainder_half, swap(remainder_half, "c", 1)),
        [VMEM] * 4,
        flops=10**6,
        nbytes=10**6,
    )
    quotient_grad = call(
        owner_kernel,
        jax.ShapeDtypeStruct((QROWS, E), F32),
        (arrived, *steps),
        [VMEM] * 4,
        [pltpu.VMEM((16, LANES), F32)],
        flops=10**9,
        nbytes=3 * 10**6,
    )
    return (quotient_grad, remainder_grad, tower_grad)


def solution(mesh):
    fine = Mesh(mesh.devices.reshape(NX, NY, NZ, NC), AXES)
    rows = P(AXES, None)
    return jax.shard_map(
        local,
        mesh=fine,
        in_specs=(rows,) * 10,
        out_specs=(rows, P(("x", "y"), None), P()),
        check_vma=False,
    )
```

```python
import jax
import jax.numpy as jnp
from jax import lax
from jax.experimental import pallas as pl
from jax.experimental.pallas import tpu as pltpu
from jax.sharding import Mesh
from jax.sharding import PartitionSpec as P

E = 256
LANES = 128
LOOK = 2048
BAGS = 1024
QCAP = 2
RCAP = 16
QROWS = 256
RROWS = 64
NX, NY, NZ, NC = 4, 8, 12, 2
GRP = NX * NY
DEVICES = GRP * NZ * NC
HID = 512
TROWS = HID // GRP
PIECE = 65
PLANE = NX * NC
SHEET = NY * NZ
CHAIN = 96
SUMS = RROWS + TROWS
F32 = jnp.float32
BF16 = jnp.bfloat16
AXES = ("x", "y", "z", "c")
VMEM = pl.BlockSpec(memory_space=pltpu.VMEM)
SMEM = pl.BlockSpec(memory_space=pltpu.SMEM)
ANY = pl.BlockSpec(memory_space=pl.ANY)


def call(body, out_shape, inputs, specs, scratch=(), flops=0, nbytes=0, room=32):
    return pl.pallas_call(
        body,
        out_shape=out_shape,
        in_specs=specs,
        out_specs=jax.tree.map(lambda _: VMEM, out_shape),
        scratch_shapes=list(scratch),
        compiler_params=pltpu.CompilerParams(vmem_limit_bytes=room * 1024 * 1024),
        cost_estimate=pl.CostEstimate(flops=flops, bytes_accessed=nbytes, transcendentals=0),
    )(*inputs)


def split_terms(bag_smem, bag_ref, pooled_ref, saved_ref, parts_ref):
    lane = lax.broadcasted_iota(jnp.int32, (LANES, LANES), 1)
    for block in range(LOOK // LANES):
        rows = pl.ds(block * LANES, LANES)
        first = jnp.minimum(bag_smem[0, block * LANES] // 16 * 16, BAGS - 2 * LANES)
        first = pl.multiple_of(first, 16)
        row = bag_ref[0:1, block * LANES : (block + 1) * LANES] - first
        column = jnp.transpose(jnp.broadcast_to(row, (LANES, LANES)).astype(F32)).astype(jnp.int32)
        pick = jnp.concatenate([column == lane, column == lane + LANES], axis=1)
        pick = jnp.where(pick, 1.0, 0.0).astype(BF16)
        gathered = jnp.dot(pick, pooled_ref[pl.ds(first, 2 * LANES), :], preferred_element_type=F32)
        terms = gathered * saved_ref[rows, :].astype(F32)
        high = terms.astype(BF16)
        parts_ref[rows, 0:E] = high
        parts_ref[rows, E:] = (terms - high.astype(F32)).astype(BF16)


def one_hot(index_row, first, count, step=1):
    number = lax.broadcasted_iota(jnp.int32, (count, index_row.shape[1]), 0) * step + first
    return jnp.where(number == index_row, 1.0, 0.0).astype(BF16)


def sums(pick, parts):
    both = jnp.dot(pick, parts, preferred_element_type=F32)
    return both[:, :E] + both[:, E:]


def small_kernel(
    bag_smem, bag_ref, slot_ref, rows_ref, qrows_ref, pooled_hbm, saved_hbm, tin_hbm, tcot_hbm, out_ref,
    pooled_ref, saved_ref, tin_ref, tcot_ref, parts_ref, arrivals,
):
    pairs = ((tin_hbm, tin_ref), (tcot_hbm, tcot_ref), (pooled_hbm, pooled_ref), (saved_hbm, saved_ref))
    copies = [pltpu.make_async_copy(src, dst, arrivals.at[k]) for k, (src, dst) in enumerate(pairs)]
    for copy in copies:
        copy.start()
    copies[0].wait()
    copies[1].wait()
    tower = lax.dot_general(tin_ref[...], tcot_ref[...], (((0,), (0,)), ((), ())), preferred_element_type=F32)
    for g in range(GRP):
        for h in range(2):
            rows = slice(g * PIECE + 32 + 16 * h, g * PIECE + 48 + 16 * h)
            out_ref[rows, :] = tower[g * TROWS : (g + 1) * TROWS, h * LANES : (h + 1) * LANES]
    labels = None
    for ref, first in ((qrows_ref, 0), (rows_ref, 48)):
        count = ref.shape[1]
        each = count // GRP
        slot = lax.broadcasted_iota(jnp.int32, (GRP, count), 1)
        group = lax.broadcasted_iota(jnp.int32, (GRP, count), 0)
        chosen = jnp.where(slot // each == group, jnp.broadcast_to(ref[...], (GRP, count)), 0).astype(F32).astype(BF16)
        slot = lax.broadcasted_iota(jnp.int32, (count, LANES), 0)
        lane = lax.broadcasted_iota(jnp.int32, (count, LANES), 1)
        spread = jnp.where(slot % each + first == lane, 1.0, 0.0).astype(BF16)
        part = jnp.dot(chosen, spread, preferred_element_type=F32)
        labels = part if labels is None else labels + part
    out_ref[pl.ds(64, GRP, stride=PIECE), :] = labels
    copies[2].wait()
    copies[3].wait()
    split_terms(bag_smem, bag_ref, pooled_ref, saved_ref, parts_ref)
    slots = slot_ref[...]
    for half in range(2):
        found = sums(one_hot(slots, half * 256, 256), parts_ref[...])
        for k in range(GRP // 2):
            first = (half * (GRP // 2) + k) * PIECE
            for h in range(2):
                rows = slice(first + 16 * h, first + 16 * h + 16)
                out_ref[rows, :] = found[k * RCAP : (k + 1) * RCAP, h * LANES : (h + 1) * LANES]


def large_kernel(bag_smem, bag_ref, pooled_ref, saved_ref, slot_ref, out_ref, parts_ref):
    split_terms(bag_smem, bag_ref, pooled_ref, saved_ref, parts_ref)
    slots = slot_ref[...]
    row = lax.broadcasted_iota(jnp.int32, (2 * SHEET, LOOK), 0)
    home = row % SHEET * 4 + row // SHEET
    for block in range(PLANE):
        first = block // NC * (4 * SHEET) + block % NC * 2
        pick = jnp.where(home == slots - first, 1.0, 0.0).astype(BF16)
        found = sums(pick, parts_ref[...])
        for h in range(2):
            out_ref[block, h * 2 * SHEET : (h + 1) * 2 * SHEET, :] = found[:, h * LANES : (h + 1) * LANES]


def turn_kernel(got_ref, out_ref):
    for source in range(PLANE):
        for h in range(2):
            for p in range(QCAP):
                rows = pl.ds(h * 16 + source * QCAP + p, SHEET, stride=32)
                first = (h * QCAP + p) * SHEET
                out_ref[rows, :] = got_ref[source, first : first + SHEET, :]


def halves(values):
    high = values.astype(BF16)
    return jnp.concatenate([high, (values - high.astype(F32)).astype(BF16)], axis=1)


def merge_kernel(got_ref, keep_ref, give_ref, onward_ref):
    known = got_ref[pl.ds(64, GRP, stride=PIECE), :].astype(BF16)
    line = lax.broadcasted_iota(jnp.int32, (LANES, GRP * RCAP), 0)
    slot = lax.broadcasted_iota(jnp.int32, (LANES, GRP * RCAP), 1)
    labels = jnp.dot(known, jnp.where(line == slot % RCAP + 48, 1.0, 0.0).astype(BF16), preferred_element_type=F32)
    source = lax.broadcasted_iota(jnp.int32, (GRP, GRP * RCAP), 0)
    slot = lax.broadcasted_iota(jnp.int32, (GRP, GRP * RCAP), 1)
    labels = jnp.sum(jnp.where(slot // RCAP == source, labels, 0.0), axis=0, keepdims=True)
    pick = one_hot(labels.astype(jnp.int32), 0, RROWS)
    core = lax.axis_index("c")
    for h in range(2):
        values = [got_ref[g * PIECE + 16 * h : g * PIECE + 16 * h + 16, :] for g in range(GRP)]
        values = jnp.concatenate(values, axis=0)
        both = jnp.dot(pick, halves(values), preferred_element_type=F32)
        remainder = both[:, :LANES] + both[:, LANES:]
        tower = sum(got_ref[g * PIECE + 32 + 16 * h : g * PIECE + 48 + 16 * h, :] for g in range(GRP))
        for kept, ref in ((True, keep_ref), (False, give_ref)):

            @pl.when((core == h) == kept)
            def _(ref=ref, remainder=remainder, tower=tower):
                ref[0:RROWS, :] = remainder
                ref[RROWS:SUMS, :] = tower

    group = lax.broadcasted_iota(jnp.int32, (GRP, LANES), 0)
    lane = lax.broadcasted_iota(jnp.int32, (GRP, LANES), 1)
    total = None
    for p in range(QCAP):
        spread = jnp.where(lane == group % NY * 16 + group // NY * 4 + core * 2 + p, 1.0, 0.0).astype(BF16)
        moved = lax.dot_general(known, spread, (((0,), (0,)), ((), ())), preferred_element_type=F32)
        row = lax.broadcasted_iota(jnp.int32, (LANES, LANES), 0)
        moved = jnp.where(row % QCAP == p, moved, 0.0)
        total = moved if total is None else total + moved
    onward_ref[...] = total
    z = lax.axis_index("z")
    for ref, c in ((keep_ref, core), (give_ref, 1 - core)):
        ref[SUMS:, :] = jnp.zeros((CHAIN - SUMS, LANES), F32)
        for i in range(NZ):
            first = lax.rem(z + i + NZ - 5, NZ) * 4 + c * 2
            at = SUMS + i % 4 * 3 + i // 4
            ref[at : at + 1, :] = onward_ref[pl.ds(first, 1), :] + onward_ref[pl.ds(first + 1, 1), :]


def near_kernel(up_ref, own_ref, down1_ref, down2_ref, out_ref):
    refs = (up_ref, own_ref, down1_ref, down2_ref)
    out_ref[0:SUMS, :] = sum(ref[0:SUMS, :] for ref in refs)
    out_ref[SUMS:, :] = jnp.zeros((CHAIN - SUMS, LANES), F32)
    for m in range(3):
        for e, ref in enumerate(refs):
            at = SUMS + 4 * m + e
            out_ref[at : at + 1, :] = ref[SUMS + 3 * e + m : SUMS + 3 * e + m + 1, :]


def pass_kernel(value_ref, after1_ref, after2_ref, out_ref):
    pass


def owner_kernel(got_ref, step0_ref, step1_ref, step2_ref, out_ref, label_ref):
    z = lax.axis_index("z")
    for m, ref in enumerate((step0_ref, step1_ref, step2_ref)):
        label_ref[4 * m : 4 * m + 4, :] = ref[SUMS + 4 * m : SUMS + 4 * m + 4, :]
    labels = [label_ref[pl.ds(lax.rem(z - source + 5 + NZ, NZ), 1), :] for source in range(NZ)]
    pick = one_hot(jnp.concatenate(labels, axis=1).astype(jnp.int32), 0, QROWS)
    for h in range(2):
        values = [
            got_ref[y * NZ + source, 16 * h : 16 * h + 16, :] for source in range(NZ) for y in range(NY)
        ]
        both = jnp.dot(pick, halves(jnp.concatenate(values, axis=0)), preferred_element_type=F32)
        out_ref[:, h * LANES : (h + 1) * LANES] = both[:, :LANES] + both[:, LANES:]


def finish_kernel(own_ref, other_ref, own_rem_ref, other_rem_ref, rem_ref, tower_ref):
    group = lax.axis_index("x") * NY + lax.axis_index("y")

    def place(own, other, left, right):
        rem_ref[:, left] = own[0][...]
        rem_ref[:, right] = other[0][...]
        for j in range(GRP):
            rows = pl.ds(pl.multiple_of(jnp.bitwise_xor(group, j) * TROWS, TROWS), TROWS)
            tower_ref[rows, left] = own[1][j * TROWS : (j + 1) * TROWS, :]
            tower_ref[rows, right] = other[1][j * TROWS : (j + 1) * TROWS, :]

    low, high = slice(0, LANES), slice(LANES, E)

    @pl.when(lax.axis_index("c") == 0)
    def _():
        place((own_rem_ref, own_ref), (other_rem_ref, other_ref), low, high)

    @pl.when(lax.axis_index("c") == 1)
    def _():
        place((own_rem_ref, own_ref), (other_rem_ref, other_ref), high, low)


def shift(value, by):
    return lax.ppermute(value, "z", [(i, (i + by) % NZ) for i in range(NZ)])


def swap(value, axis, bit):
    return lax.ppermute(value, axis, [(i, i ^ bit) for i in range(lax.axis_size(axis))])


def local(
    pooled_grad,
    lookup_bag,
    saved_quotient,
    saved_remainder,
    quotient_slot,
    quotient_rows,
    remainder_slot,
    remainder_rows,
    tower_inputs,
    tower_cotangent,
):
    parts = pltpu.VMEM((LOOK, 2 * E), BF16)
    pieces = call(
        small_kernel,
        jax.ShapeDtypeStruct((GRP * PIECE, LANES), F32),
        (lookup_bag, lookup_bag, remainder_slot, remainder_rows, quotient_rows, pooled_grad, saved_quotient, tower_inputs, tower_cotangent),
        [SMEM] + [VMEM] * 4 + [ANY] * 4,
        [
            pltpu.VMEM(pooled_grad.shape, BF16),
            pltpu.VMEM(saved_quotient.shape, BF16),
            pltpu.VMEM(tower_inputs.shape, BF16),
            pltpu.VMEM(tower_cotangent.shape, BF16),
            parts,
            pltpu.SemaphoreType.DMA((4,)),
        ],
        flops=2 * 10**9,
        nbytes=3 * 10**6,
        room=56,
    )
    pieces = pieces.reshape(GRP, 1, PIECE * LANES)
    got = lax.all_to_all(pieces, ("x", "y"), split_axis=0, concat_axis=0, tiled=True)
    outgoing = call(
        large_kernel,
        jax.ShapeDtypeStruct((PLANE, 4 * SHEET, LANES), F32),
        (lookup_bag, lookup_bag, pooled_grad, saved_remainder, quotient_slot),
        [SMEM] + [VMEM] * 4,
        [parts],
        flops=8 * 10**9,
        nbytes=5 * 10**6,
    )
    across = lax.all_to_all(outgoing, ("x", "c"), split_axis=0, concat_axis=0, tiled=True)

    chain = jax.ShapeDtypeStruct((CHAIN, LANES), F32)
    keep, give = call(
        merge_kernel,
        (chain, chain),
        (got.reshape(GRP * PIECE, LANES),),
        [VMEM],
        [pltpu.VMEM((LANES, LANES), F32)],
        flops=10**8,
        nbytes=2 * 10**6,
    )
    keep = keep + swap(give, "c", 1)
    step = call(
        near_kernel,
        chain,
        (shift(keep, -1), keep, shift(keep, 1), shift(keep, 2)),
        [VMEM] * 4,
        flops=10**5,
        nbytes=10**5,
    )
    steps = (shift(step, -4), step, shift(step, 4))
    total = sum(value[:SUMS] for value in steps)

    turned = call(
        turn_kernel,
        jax.ShapeDtypeStruct((SHEET * 32, LANES), F32),
        (across,),
        [VMEM],
        flops=10**7,
        nbytes=4 * 10**6,
    )
    turned = pl.pallas_call(
        pass_kernel,
        out_shape=jax.ShapeDtypeStruct((SHEET * 32, LANES), F32),
        in_specs=[ANY] * 3,
        out_specs=ANY,
        input_output_aliases={0: 0},
    )(turned, steps[0], steps[2])
    arrived = lax.all_to_all(turned.reshape(SHEET, 32, LANES), ("y", "z"), split_axis=0, concat_axis=0, tiled=True)

    remainder_half, tower_half = total[:RROWS], total[RROWS:]
    for axis, bits in (("y", (1, 2, 4)), ("x", (1, 2))):
        for bit in bits:
            tower_half = jnp.concatenate([tower_half, swap(tower_half, axis, bit)], axis=0)
    remainder_grad, tower_grad = call(
        finish_kernel,
        (jax.ShapeDtypeStruct((RROWS, E), F32), jax.ShapeDtypeStruct((HID, E), F32)),
        (tower_half, swap(tower_half, "c", 1), remainder_half, swap(remainder_half, "c", 1)),
        [VMEM] * 4,
        flops=10**6,
        nbytes=10**6,
    )
    quotient_grad = call(
        owner_kernel,
        jax.ShapeDtypeStruct((QROWS, E), F32),
        (arrived, *steps),
        [VMEM] * 4,
        [pltpu.VMEM((16, LANES), F32)],
        flops=10**9,
        nbytes=3 * 10**6,
    )
    return (quotient_grad, remainder_grad, tower_grad)


def solution(mesh):
    fine = Mesh(mesh.devices.reshape(NX, NY, NZ, NC), AXES)
    rows = P(AXES, None)
    return jax.shard_map(
        local,
        mesh=fine,
        in_specs=(rows,) * 10,
        out_specs=(rows, P(("x", "y"), None), P()),
        check_vma=False,
    )
```

```python
import jax
import jax.numpy as jnp
from jax import lax
from jax.experimental import pallas as pl
from jax.experimental.pallas import tpu as pltpu
from jax.sharding import Mesh
from jax.sharding import PartitionSpec as P

E = 256
LANES = 128
LOOK = 2048
BAGS = 1024
QCAP = 2
RCAP = 16
QROWS = 256
RROWS = 64
NX, NY, NZ, NC = 4, 8, 12, 2
GRP = NX * NY
DEVICES = GRP * NZ * NC
HID = 512
TROWS = HID // GRP
PIECE = 65
PLANE = NX * NC
SHEET = NY * NZ
CHAIN = 96
SUMS = RROWS + TROWS
F32 = jnp.float32
BF16 = jnp.bfloat16
AXES = ("x", "y", "z", "c")
VMEM = pl.BlockSpec(memory_space=pltpu.VMEM)
SMEM = pl.BlockSpec(memory_space=pltpu.SMEM)
ANY = pl.BlockSpec(memory_space=pl.ANY)


def call(body, out_shape, inputs, specs, scratch=(), flops=0, nbytes=0, room=32):
    return pl.pallas_call(
        body,
        out_shape=out_shape,
        in_specs=specs,
        out_specs=jax.tree.map(lambda _: VMEM, out_shape),
        scratch_shapes=list(scratch),
        compiler_params=pltpu.CompilerParams(vmem_limit_bytes=room * 1024 * 1024),
        cost_estimate=pl.CostEstimate(flops=flops, bytes_accessed=nbytes, transcendentals=0),
    )(*inputs)


def split_terms(bag_smem, bag_ref, pooled_ref, saved_ref, parts_ref):
    lane = lax.broadcasted_iota(jnp.int32, (LANES, LANES), 1)
    for block in range(LOOK // LANES):
        rows = pl.ds(block * LANES, LANES)
        first = jnp.minimum(bag_smem[0, block * LANES] // 16 * 16, BAGS - 2 * LANES)
        first = pl.multiple_of(first, 16)
        row = bag_ref[0:1, block * LANES : (block + 1) * LANES] - first
        column = jnp.transpose(jnp.broadcast_to(row, (LANES, LANES)).astype(F32)).astype(jnp.int32)
        pick = jnp.concatenate([column == lane, column == lane + LANES], axis=1)
        pick = jnp.where(pick, 1.0, 0.0).astype(BF16)
        gathered = jnp.dot(pick, pooled_ref[pl.ds(first, 2 * LANES), :], preferred_element_type=F32)
        terms = gathered * saved_ref[rows, :].astype(F32)
        high = terms.astype(BF16)
        parts_ref[rows, 0:E] = high
        parts_ref[rows, E:] = (terms - high.astype(F32)).astype(BF16)


def one_hot(index_row, first, count, step=1):
    number = lax.broadcasted_iota(jnp.int32, (count, index_row.shape[1]), 0) * step + first
    return jnp.where(number == index_row, 1.0, 0.0).astype(BF16)


def sums(pick, parts):
    both = jnp.dot(pick, parts, preferred_element_type=F32)
    return both[:, :E] + both[:, E:]


def small_kernel(
    bag_smem, bag_ref, slot_ref, rows_ref, qrows_ref, pooled_hbm, saved_hbm, tin_hbm, tcot_hbm, out_ref,
    pooled_ref, saved_ref, tin_ref, tcot_ref, parts_ref, arrivals,
):
    pairs = ((tin_hbm, tin_ref), (tcot_hbm, tcot_ref), (pooled_hbm, pooled_ref), (saved_hbm, saved_ref))
    copies = [pltpu.make_async_copy(src, dst, arrivals.at[k]) for k, (src, dst) in enumerate(pairs)]
    for copy in copies:
        copy.start()
    labels = None
    for ref, first in ((qrows_ref, 0), (rows_ref, 48)):
        count = ref.shape[1]
        each = count // GRP
        slot = lax.broadcasted_iota(jnp.int32, (GRP, count), 1)
        group = lax.broadcasted_iota(jnp.int32, (GRP, count), 0)
        chosen = jnp.where(slot // each == group, jnp.broadcast_to(ref[...], (GRP, count)), 0).astype(F32).astype(BF16)
        slot = lax.broadcasted_iota(jnp.int32, (count, LANES), 0)
        lane = lax.broadcasted_iota(jnp.int32, (count, LANES), 1)
        spread = jnp.where(slot % each + first == lane, 1.0, 0.0).astype(BF16)
        part = jnp.dot(chosen, spread, preferred_element_type=F32)
        labels = part if labels is None else labels + part
    out_ref[pl.ds(64, GRP, stride=PIECE), :] = labels
    copies[0].wait()
    copies[1].wait()
    tower = lax.dot_general(tin_ref[...], tcot_ref[...], (((0,), (0,)), ((), ())), preferred_element_type=F32)
    for g in range(GRP):
        for h in range(2):
            rows = slice(g * PIECE + 32 + 16 * h, g * PIECE + 48 + 16 * h)
            out_ref[rows, :] = tower[g * TROWS : (g + 1) * TROWS, h * LANES : (h + 1) * LANES]
    copies[2].wait()
    copies[3].wait()
    split_terms(bag_smem, bag_ref, pooled_ref, saved_ref, parts_ref)
    slots = slot_ref[...]
    for half in range(2):
        found = sums(one_hot(slots, half * 256, 256), parts_ref[...])
        for k in range(GRP // 2):
            first = (half * (GRP // 2) + k) * PIECE
            for h in range(2):
                rows = slice(first + 16 * h, first + 16 * h + 16)
                out_ref[rows, :] = found[k * RCAP : (k + 1) * RCAP, h * LANES : (h + 1) * LANES]


def large_kernel(bag_smem, bag_ref, pooled_ref, saved_ref, slot_ref, out_ref, parts_ref):
    split_terms(bag_smem, bag_ref, pooled_ref, saved_ref, parts_ref)
    slots = slot_ref[...]
    row = lax.broadcasted_iota(jnp.int32, (2 * SHEET, LOOK), 0)
    home = row % SHEET * 4 + row // SHEET
    for block in range(PLANE):
        first = block // NC * (4 * SHEET) + block % NC * 2
        pick = jnp.where(home == slots - first, 1.0, 0.0).astype(BF16)
        found = sums(pick, parts_ref[...])
        for h in range(2):
            out_ref[block, h * 2 * SHEET : (h + 1) * 2 * SHEET, :] = found[:, h * LANES : (h + 1) * LANES]


def turn_kernel(got_ref, out_ref):
    for source in range(PLANE):
        for h in range(2):
            for p in range(QCAP):
                rows = pl.ds(h * 16 + source * QCAP + p, SHEET, stride=32)
                first = (h * QCAP + p) * SHEET
                out_ref[rows, :] = got_ref[source, first : first + SHEET, :]


def halves(values):
    high = values.astype(BF16)
    return jnp.concatenate([high, (values - high.astype(F32)).astype(BF16)], axis=1)


def merge_kernel(got_ref, keep_ref, give_ref, onward_ref):
    known = got_ref[pl.ds(64, GRP, stride=PIECE), :].astype(BF16)
    line = lax.broadcasted_iota(jnp.int32, (LANES, GRP * RCAP), 0)
    slot = lax.broadcasted_iota(jnp.int32, (LANES, GRP * RCAP), 1)
    labels = jnp.dot(known, jnp.where(line == slot % RCAP + 48, 1.0, 0.0).astype(BF16), preferred_element_type=F32)
    source = lax.broadcasted_iota(jnp.int32, (GRP, GRP * RCAP), 0)
    slot = lax.broadcasted_iota(jnp.int32, (GRP, GRP * RCAP), 1)
    labels = jnp.sum(jnp.where(slot // RCAP == source, labels, 0.0), axis=0, keepdims=True)
    pick = one_hot(labels.astype(jnp.int32), 0, RROWS)
    core = lax.axis_index("c")
    for h in range(2):
        values = [got_ref[g * PIECE + 16 * h : g * PIECE + 16 * h + 16, :] for g in range(GRP)]
        values = jnp.concatenate(values, axis=0)
        both = jnp.dot(pick, halves(values), preferred_element_type=F32)
        remainder = both[:, :LANES] + both[:, LANES:]
        tower = sum(got_ref[g * PIECE + 32 + 16 * h : g * PIECE + 48 + 16 * h, :] for g in range(GRP))
        for kept, ref in ((True, keep_ref), (False, give_ref)):

            @pl.when((core == h) == kept)
            def _(ref=ref, remainder=remainder, tower=tower):
                ref[0:RROWS, :] = remainder
                ref[RROWS:SUMS, :] = tower

    group = lax.broadcasted_iota(jnp.int32, (GRP, LANES), 0)
    lane = lax.broadcasted_iota(jnp.int32, (GRP, LANES), 1)
    total = None
    for p in range(QCAP):
        spread = jnp.where(lane == group % NY * 16 + group // NY * 4 + core * 2 + p, 1.0, 0.0).astype(BF16)
        moved = lax.dot_general(known, spread, (((0,), (0,)), ((), ())), preferred_element_type=F32)
        row = lax.broadcasted_iota(jnp.int32, (LANES, LANES), 0)
        moved = jnp.where(row % QCAP == p, moved, 0.0)
        total = moved if total is None else total + moved
    onward_ref[...] = total
    z = lax.axis_index("z")
    for ref, c in ((keep_ref, core), (give_ref, 1 - core)):
        ref[SUMS:, :] = jnp.zeros((CHAIN - SUMS, LANES), F32)
        for i in range(NZ):
            first = lax.rem(z + i + NZ - 5, NZ) * 4 + c * 2
            at = SUMS + i % 4 * 3 + i // 4
            ref[at : at + 1, :] = onward_ref[pl.ds(first, 1), :] + onward_ref[pl.ds(first + 1, 1), :]


def near_kernel(up_ref, own_ref, down1_ref, down2_ref, out_ref):
    refs = (up_ref, own_ref, down1_ref, down2_ref)
    out_ref[0:SUMS, :] = sum(ref[0:SUMS, :] for ref in refs)
    out_ref[SUMS:, :] = jnp.zeros((CHAIN - SUMS, LANES), F32)
    for m in range(3):
        for e, ref in enumerate(refs):
            at = SUMS + 4 * m + e
            out_ref[at : at + 1, :] = ref[SUMS + 3 * e + m : SUMS + 3 * e + m + 1, :]


def pass_kernel(value_ref, after1_ref, after2_ref, out_ref):
    pass


def owner_kernel(got_ref, step0_ref, step1_ref, step2_ref, out_ref, label_ref):
    z = lax.axis_index("z")
    for m, ref in enumerate((step0_ref, step1_ref, step2_ref)):
        label_ref[4 * m : 4 * m + 4, :] = ref[SUMS + 4 * m : SUMS + 4 * m + 4, :]
    labels = [label_ref[pl.ds(lax.rem(z - source + 5 + NZ, NZ), 1), :] for source in range(NZ)]
    pick = one_hot(jnp.concatenate(labels, axis=1).astype(jnp.int32), 0, QROWS)
    for h in range(2):
        values = [
            got_ref[y * NZ + source, 16 * h : 16 * h + 16, :] for source in range(NZ) for y in range(NY)
        ]
        both = jnp.dot(pick, halves(jnp.concatenate(values, axis=0)), preferred_element_type=F32)
        out_ref[:, h * LANES : (h + 1) * LANES] = both[:, :LANES] + both[:, LANES:]


def finish_kernel(own_ref, other_ref, own_rem_ref, other_rem_ref, rem_ref, tower_ref):
    group = lax.axis_index("x") * NY + lax.axis_index("y")

    def place(own, other, left, right):
        rem_ref[:, left] = own[0][...]
        rem_ref[:, right] = other[0][...]
        for j in range(GRP):
            rows = pl.ds(pl.multiple_of(jnp.bitwise_xor(group, j) * TROWS, TROWS), TROWS)
            tower_ref[rows, left] = own[1][j * TROWS : (j + 1) * TROWS, :]
            tower_ref[rows, right] = other[1][j * TROWS : (j + 1) * TROWS, :]

    low, high = slice(0, LANES), slice(LANES, E)

    @pl.when(lax.axis_index("c") == 0)
    def _():
        place((own_rem_ref, own_ref), (other_rem_ref, other_ref), low, high)

    @pl.when(lax.axis_index("c") == 1)
    def _():
        place((own_rem_ref, own_ref), (other_rem_ref, other_ref), high, low)


def shift(value, by):
    return lax.ppermute(value, "z", [(i, (i + by) % NZ) for i in range(NZ)])


def swap(value, axis, bit):
    return lax.ppermute(value, axis, [(i, i ^ bit) for i in range(lax.axis_size(axis))])


def local(
    pooled_grad,
    lookup_bag,
    saved_quotient,
    saved_remainder,
    quotient_slot,
    quotient_rows,
    remainder_slot,
    remainder_rows,
    tower_inputs,
    tower_cotangent,
):
    parts = pltpu.VMEM((LOOK, 2 * E), BF16)
    pieces = call(
        small_kernel,
        jax.ShapeDtypeStruct((GRP * PIECE, LANES), F32),
        (lookup_bag, lookup_bag, remainder_slot, remainder_rows, quotient_rows, pooled_grad, saved_quotient, tower_inputs, tower_cotangent),
        [SMEM] + [VMEM] * 4 + [ANY] * 4,
        [
            pltpu.VMEM(pooled_grad.shape, BF16),
            pltpu.VMEM(saved_quotient.shape, BF16),
            pltpu.VMEM(tower_inputs.shape, BF16),
            pltpu.VMEM(tower_cotangent.shape, BF16),
            parts,
            pltpu.SemaphoreType.DMA((4,)),
        ],
        flops=2 * 10**9,
        nbytes=3 * 10**6,
        room=56,
    )
    pieces = pieces.reshape(GRP, 1, PIECE * LANES)
    got = lax.all_to_all(pieces, ("x", "y"), split_axis=0, concat_axis=0, tiled=True)
    outgoing = call(
        large_kernel,
        jax.ShapeDtypeStruct((PLANE, 4 * SHEET, LANES), F32),
        (lookup_bag, lookup_bag, pooled_grad, saved_remainder, quotient_slot),
        [SMEM] + [VMEM] * 4,
        [parts],
        flops=8 * 10**9,
        nbytes=5 * 10**6,
    )
    across = lax.all_to_all(outgoing, ("x", "c"), split_axis=0, concat_axis=0, tiled=True)

    chain = jax.ShapeDtypeStruct((CHAIN, LANES), F32)
    keep, give = call(
        merge_kernel,
        (chain, chain),
        (got.reshape(GRP * PIECE, LANES),),
        [VMEM],
        [pltpu.VMEM((LANES, LANES), F32)],
        flops=10**8,
        nbytes=2 * 10**6,
    )
    keep = keep + swap(give, "c", 1)
    step = call(
        near_kernel,
        chain,
        (shift(keep, -1), keep, shift(keep, 1), shift(keep, 2)),
        [VMEM] * 4,
        flops=10**5,
        nbytes=10**5,
    )
    steps = (shift(step, -4), step, shift(step, 4))
    total = sum(value[:SUMS] for value in steps)

    turned = call(
        turn_kernel,
        jax.ShapeDtypeStruct((SHEET * 32, LANES), F32),
        (across,),
        [VMEM],
        flops=10**7,
        nbytes=4 * 10**6,
    )
    turned = pl.pallas_call(
        pass_kernel,
        out_shape=jax.ShapeDtypeStruct((SHEET * 32, LANES), F32),
        in_specs=[ANY, VMEM, VMEM],
        out_specs=ANY,
        input_output_aliases={0: 0},
    )(turned, steps[0], steps[2])
    arrived = lax.all_to_all(turned.reshape(SHEET, 32, LANES), ("y", "z"), split_axis=0, concat_axis=0, tiled=True)

    remainder_half, tower_half = total[:RROWS], total[RROWS:]
    for axis, bits in (("y", (1, 2, 4)), ("x", (1, 2))):
        for bit in bits:
            tower_half = jnp.concatenate([tower_half, swap(tower_half, axis, bit)], axis=0)
    remainder_grad, tower_grad = call(
        finish_kernel,
        (jax.ShapeDtypeStruct((RROWS, E), F32), jax.ShapeDtypeStruct((HID, E), F32)),
        (tower_half, swap(tower_half, "c", 1), remainder_half, swap(remainder_half, "c", 1)),
        [VMEM] * 4,
        flops=10**6,
        nbytes=10**6,
    )
    quotient_grad = call(
        owner_kernel,
        jax.ShapeDtypeStruct((QROWS, E), F32),
        (arrived, *steps),
        [VMEM] * 4,
        [pltpu.VMEM((16, LANES), F32)],
        flops=10**9,
        nbytes=3 * 10**6,
    )
    return (quotient_grad, remainder_grad, tower_grad)


def solution(mesh):
    fine = Mesh(mesh.devices.reshape(NX, NY, NZ, NC), AXES)
    rows = P(AXES, None)
    return jax.shard_map(
        local,
        mesh=fine,
        in_specs=(rows,) * 10,
        out_specs=(rows, P(("x", "y"), None), P()),
        check_vma=False,
    )
```
